256 devices in a mesh: seq: 64 (over y, z, core), chan: 4 (over x).
Axes of the slice: x: 4, y: 4, z: 8, core: 2. Of those that a mesh axis runs over, the one named last changes fastest.
Arguments:
- inputs: bfloat16 [8192, 4096], P('seq', 'chan'), may hold values from -6 to 6
- grads: bfloat16 [8192, 4096], P('seq', 'chan'), may hold values from -0.15625 to 0.15625
- filter_taps: float32 [512, 4096], P(('seq', 'chan')), may hold values from -6 to 6
- supports: int32 [32], replicated, may hold values from 1 to 4, as said below
Outputs:
- grad_inputs: bfloat16 [8192, 4096], P('seq', 'chan')
- grad_filter: float32 [512, 4096], P(('seq', 'chan'))
The draws below stay inside these ranges and needn't reach their ends.
Inputs may be any that keep to these rules, and one draw needn't show every extreme that they name: `supports`: some group spans 4 blocks and some group spans 1 block.
All inputs are finite; a program needn't handle non-finite values.
Results may differ from the reference program's by a relative error of at most 0.001.
Values may be sent and summed in bfloat16 or wider, within the bound.
A program may use at most 64 MiB of HBM per device.

```python
import jax
import jax.numpy as jnp

TB = 128
GROUP_CH = 128
GROUPS = 32
CHANNELS = 4096
SEQ = 8192
SMAX = 4
LAGS = 512


def draw_supports(key, part):
    key = jax.random.fold_in(key, 1)
    values = jax.random.randint(jax.random.fold_in(key, 2), (GROUPS,), 1, SMAX + 1).astype(jnp.int32)
    order = jax.random.permutation(jax.random.fold_in(key, 3), GROUPS)
    values = values.at[order[0]].set(SMAX)
    values = values.at[order[1]].set(1)
    return values.astype(jnp.int32)


def block_scale(key, dims, cuts, least, largest):
    factor_of, own = 1.0, jax.random.fold_in(key, 6)
    for axis_at, shards_of in cuts:
        steps = jnp.exp(jax.random.uniform(jax.random.fold_in(own, axis_at), (shards_of,), jnp.float32, least / len(cuts), largest / len(cuts)))
        factor_of = factor_of * jnp.repeat(steps, dims[axis_at] // shards_of).reshape([-1 if axis == axis_at else 1 for axis in range(len(dims))])
    return factor_of


def normal_values(own_key, shape, deviation, bound, split=(), kind=jnp.bfloat16):
    gain = block_scale(own_key, shape, split, -0.22, 0.18) if split else 1.0
    entries = jax.random.normal(own_key, shape, jnp.float32) * deviation * gain
    return jnp.minimum(jnp.maximum(entries, -bound), bound).astype(kind)


def setup_inputs(seed: int = 0) -> dict:
    splits = jax.random.split(jax.random.key(seed), 5)
    inputs = normal_values(splits[0], (SEQ, CHANNELS), 1.0, 6.0, ((0, 64), (1, 4)))
    grads = normal_values(splits[1], (SEQ, CHANNELS), (SEQ ** -0.5), 0.15625, ((0, 64), (1, 4)))
    filter_taps = normal_values(splits[2], (LAGS, CHANNELS), 1.0, 6.0, ((0, 256),), jnp.float32)
    supports = draw_supports(jax.random.fold_in(splits[4], 71), 0)
    return {"inputs": inputs, "grads": grads, "filter_taps": filter_taps, "supports": supports}


def reference(inputs, grads, filter_taps, supports):
    limit = jnp.repeat(supports, GROUP_CH) * TB
    lag_pos = jnp.arange(LAGS, dtype=jnp.int32)[:, None]
    taps = jnp.where(lag_pos < limit[None, :], filter_taps, jnp.zeros_like(filter_taps))
    signal = inputs.astype(jnp.float32)
    upstream = grads.astype(jnp.float32)
    span_len = 2 * SEQ
    grad_spec = jnp.fft.rfft(upstream, n=span_len, axis=0)
    tap_spec = jnp.fft.rfft(taps, n=span_len, axis=0)
    signal_spec = jnp.fft.rfft(signal, n=span_len, axis=0)
    grad_inputs = jnp.fft.irfft(grad_spec * jnp.conj(tap_spec), n=span_len, axis=0)[:SEQ]
    corr = jnp.fft.irfft(grad_spec * jnp.conj(signal_spec), n=span_len, axis=0)[:LAGS]
    grad_filter = jnp.where(lag_pos < limit[None, :], corr, jnp.zeros_like(corr))
    return grad_inputs.astype(jnp.bfloat16), grad_filter.astype(jnp.float32)
```

```python
import functools

import jax
import jax.numpy as jnp
from jax import lax
from jax.experimental import pallas as pl
from jax.experimental.pallas import tpu as pltpu
from jax.sharding import PartitionSpec as P

MESH = pl.DeviceIdType.MESH
F32 = jnp.float32
BF16 = jnp.bfloat16
TB = 128
SMAX = 4
SEQ_DEV = 64
CHAN_DEV = 4
WIDTH = 1024
OWN = 16
LAGS = SMAX * TB
SPAN = LAGS + TB
ROWS = SEQ_DEV * OWN
NT = (((1,), (1,)), ((), ()))


def iota(shape, axis):
    return lax.broadcasted_iota(jnp.int32, shape, axis)


def high_low(value):
    high = value.astype(BF16)
    return jnp.concatenate([high, (value - high.astype(F32)).astype(BF16)], axis=0)


def take_all(landed, send_sem, recv_sem, count):
    span = landed.at[pl.ds(0, count)]
    pltpu.make_async_copy(span, span, recv_sem).wait()
    pltpu.make_async_copy(span, span, send_sem).wait()


def spread(source, landed, send_sem, recv_sem, me):
    def one(step, carry):
        to = lax.rem(me + step, SEQ_DEV)
        pltpu.make_async_remote_copy(
            source.at[pl.ds(to, 1)], landed.at[pl.ds(me, 1)], send_sem, recv_sem, device_id={"seq": to}, device_id_type=MESH
        ).start()
        return carry

    lax.fori_loop(1, SEQ_DEV, one, 0)


def turn(block_ref, out_ref, backwards):
    mirror = jnp.where(iota((TB, TB), 0) + iota((TB, TB), 1) == TB - 1, 1.0, 0.0).astype(BF16)
    for tile in range(WIDTH // 128):
        flipped = block_ref[:, tile * 128 : (tile + 1) * 128].astype(F32).T.astype(BF16)
        if backwards:
            flipped = jnp.dot(flipped, mirror, preferred_element_type=F32).astype(BF16)
        out_ref[tile * 8 : (tile + 1) * 8] = flipped.reshape(8, OWN, 128)


def kernel(
    supports, grads, inputs, taps, gi_out, gf_out,
    g_here, x_here, t_here, g_send, x_send, g_land, x_land, gi_send,
    t_first, t_rows, row_send, row_land, g_wide, x_wide, gi_wide, toeplitz, windows, tap_lines, partial,
    order, back_send, back_land, last_send, last_land,
    in_sem, send_sem, recv_sem, local_sem,
):
    me, chan = lax.axis_index("seq"), lax.axis_index("chan")
    phase = lax.rem(me, 8)
    load_g = pltpu.make_async_copy(grads, g_here, in_sem.at[0])
    load_t = pltpu.make_async_copy(taps, t_here, in_sem.at[1])
    load_x = pltpu.make_async_copy(inputs, x_here, in_sem.at[2])
    load_g.start()
    load_t.start()
    load_x.start()

    barrier = pltpu.get_barrier_semaphore()

    def greet(step, carry):
        pl.semaphore_signal(barrier, inc=1, device_id={"seq": lax.rem(me + step, SEQ_DEV)}, device_id_type=MESH)
        return carry

    lax.fori_loop(1, SEQ_DEV, greet, 0)
    for step in range(1, CHAN_DEV):
        pl.semaphore_signal(barrier, inc=1, device_id={"chan": lax.rem(chan + step, CHAN_DEV)}, device_id_type=MESH)

    load_g.wait()
    turn(g_here, g_send, False)
    load_t.wait()
    pl.semaphore_wait(barrier, SEQ_DEV - 1 + CHAN_DEV - 1)

    for step in range(1, CHAN_DEV):
        to = lax.rem(chan + step, CHAN_DEV)
        pltpu.make_async_remote_copy(
            t_here.at[:, pl.ds(pl.multiple_of(to * WIDTH, WIDTH), WIDTH)], t_first.at[chan],
            send_sem.at[0], recv_sem.at[0], device_id={"chan": to}, device_id_type=MESH,
        ).start()
    spread(g_send, g_land, send_sem.at[1], recv_sem.at[1], me)
    g_land[me] = g_send[me]
    t_first[chan] = t_here[:, pl.ds(pl.multiple_of(chan * WIDTH, WIDTH), WIDTH)]
    load_x.wait()
    turn(x_here, x_send, True)
    x_land[me] = x_send[me]

    row = iota((512, 1), 0)
    group = ((row // 64) % 2) * 4 + row // 128
    lag_of = (row % 64) * 8 + ((phase + 8 - group) & 7)
    order[...] = jnp.where(iota((512, LAGS), 1) == lag_of, 1.0, 0.0).astype(BF16)
    lane_group, sublane = iota((8, 128), 1) // 16, iota((8, 128), 0)

    take_all(t_first, send_sem.at[0], recv_sem.at[0], CHAN_DEV - 1)
    for x in range(CHAN_DEV):
        t_rows[2 * x : 2 * x + 2, :] = t_first[x]
    for tile in range(8):
        block = t_rows[:, tile * 128 : (tile + 1) * 128]
        skewed = block
        for r in range(1, 8):
            skewed = jnp.where(sublane == r, pltpu.roll(block, 128 - 16 * r, axis=1), skewed)
        moved = skewed
        for k in range(1, 8):
            moved = jnp.where(lane_group == k, pltpu.roll(skewed, k, axis=0), moved)
        row_send[tile * 8 : (tile + 1) * 8, :] = moved
    spread(row_send, row_land, send_sem.at[2], recv_sem.at[2], me)
    row_land[pl.ds(me, 1), :] = row_send[pl.ds(me, 1), :]
    spread(x_send, x_land, send_sem.at[3], recv_sem.at[3], me)

    g_wide[ROWS:, :] = jnp.zeros((SMAX * OWN, 128), F32)
    own_lags = TB * supports[chan * (WIDTH // 128) + me // 8]

    take_all(row_land, send_sem.at[2], recv_sem.at[2], SEQ_DEV - 1)
    landed = row_land[...]
    flipped = jnp.concatenate([landed, pltpu.roll(landed, 64, axis=1)], axis=0).T
    placed = jnp.concatenate([flipped[16 * q : 16 * q + 16] for q in range(4)], axis=1)
    both = jnp.dot(high_low(placed), order[...], preferred_element_type=F32)
    own_taps = jnp.where(iota((OWN, LAGS), 1) < own_lags, both[:OWN] + both[OWN:], 0.0)
    tap_lines[...] = own_taps

    below = iota((TB, TB), 1) >= iota((TB, TB), 0)

    def build(c, carry):
        line = tap_lines[pl.ds(c, 1), :]
        before = jnp.zeros((TB, TB), F32)
        for j in range(SMAX + 1):
            if j < SMAX:
                now = jnp.broadcast_to(line[:, j * TB : (j + 1) * TB], (TB, TB))
                now = pltpu.roll(now, 0, axis=1, stride=1, stride_axis=0)
            else:
                now = jnp.zeros((TB, TB), F32)
            toeplitz[c, :, j * TB : (j + 1) * TB] = high_low(jnp.where(below, now, before))
            before = now
        return carry

    lax.fori_loop(0, OWN, build, 0)

    take_all(g_land, send_sem.at[1], recv_sem.at[1], SEQ_DEV - 1)
    g_wide[0:ROWS, :] = g_land[...].reshape(ROWS, 128).astype(F32)

    def signal_back(c, carry):
        for j in range(SMAX + 1):
            windows[c, :, j * TB : (j + 1) * TB] = g_wide[pl.ds(j * OWN + c, SEQ_DEV, stride=OWN), :].astype(BF16)
        both = lax.dot_general(windows[c], toeplitz[c], NT, preferred_element_type=F32)
        gi_wide[pl.ds(c, SEQ_DEV, stride=OWN), :] = both[:, :TB] + both[:, TB:]
        return carry

    lax.fori_loop(0, OWN, signal_back, 0)
    gi_send[...] = gi_wide[...].astype(BF16).reshape(SEQ_DEV, OWN, 128)
    spread(gi_send, gi_out, send_sem.at[4], recv_sem.at[4], me)
    keep = pltpu.make_async_copy(gi_send.at[pl.ds(me, 1)], gi_out.at[pl.ds(me, 1)], local_sem)
    keep.start()

    take_all(x_land, send_sem.at[3], recv_sem.at[3], SEQ_DEV - 1)
    x_wide[...] = x_land[...].reshape(ROWS, 128).astype(F32)
    inside = iota((TB, TB), 1) <= iota((TB, TB), 0)

    def lag_sums(c, carry):
        signal = x_wide[pl.ds(c, SEQ_DEV, stride=OWN), :].T.astype(BF16)
        after = None
        for j in range(SMAX, -1, -1):
            product = jnp.dot(signal, windows[c, :, j * TB : (j + 1) * TB], preferred_element_type=F32)
            now = pltpu.roll(product, 1, axis=1, stride=1, stride_axis=0)
            if j < SMAX:
                lined = jnp.where(inside, now, after)
                partial[j, pl.ds(c * 8, 8), :] = jnp.sum(lined.reshape(TB // 8, 8, TB), axis=0)
            after = now
        return carry

    lax.fori_loop(0, OWN, lag_sums, 0)
    blocks = []
    for j in range(SMAX):
        added = partial[j, pl.ds(0, OWN, stride=8), :]
        for q in range(1, 8):
            added = added + partial[j, pl.ds(q, OWN, stride=8), :]
        blocks.append(added)
    sums = jnp.concatenate(blocks, axis=1)
    sums = jnp.where(iota((OWN, LAGS), 1) < own_lags, sums, 0.0)
    both = lax.dot_general(high_low(sums), order[...], NT, preferred_element_type=F32)
    placed = both[:OWN] + both[OWN:]
    stacked = jnp.concatenate([placed[:, q * 128 : (q + 1) * 128] for q in range(4)], axis=0)
    flipped = jnp.concatenate([stacked, stacked], axis=0).T
    back_send[...] = jnp.where(iota((64, 128), 1) < 64, flipped[:64], flipped[64:])
    spread(back_send, back_land, send_sem.at[5], recv_sem.at[5], me)
    back_land[pl.ds(me, 1), :] = back_send[pl.ds(me, 1), :]
    take_all(back_land, send_sem.at[5], recv_sem.at[5], SEQ_DEV - 1)
    for tile in range(8):
        block = back_land[tile * 8 : (tile + 1) * 8, :]
        moved = block
        for k in range(1, 8):
            moved = jnp.where(lane_group == k, pltpu.roll(block, 8 - k, axis=0), moved)
        t_rows[:, tile * 128 : (tile + 1) * 128] = pltpu.roll(moved, 0, axis=1, stride=16, stride_axis=0)
    for x in range(CHAN_DEV):
        last_send[x] = t_rows[2 * x : 2 * x + 2, :]
    for step in range(1, CHAN_DEV):
        to = lax.rem(chan + step, CHAN_DEV)
        pltpu.make_async_remote_copy(
            last_send.at[to], last_land.at[chan], send_sem.at[6], recv_sem.at[6], device_id={"chan": to}, device_id_type=MESH
        ).start()
    last_land[chan] = last_send[chan]
    take_all(last_land, send_sem.at[6], recv_sem.at[6], CHAN_DEV - 1)
    for x in range(CHAN_DEV):
        gf_out[:, x * WIDTH : (x + 1) * WIDTH] = last_land[x]
    keep.wait()
    take_all(gi_out, send_sem.at[4], recv_sem.at[4], SEQ_DEV - 1)


def finish(gi_rows, gf_here, gi, gf):
    for tile in range(WIDTH // 128):
        lanes = slice(tile * 128, (tile + 1) * 128)
        gi[:, lanes] = gi_rows[lanes, :].astype(F32).T.astype(BF16)
    gf[...] = gf_here[...]


def body(inputs, grads, filter_taps, supports):
    vmem = pl.BlockSpec(memory_space=pltpu.VMEM)
    anywhere = pl.BlockSpec(memory_space=pl.ANY)
    blocks = (SEQ_DEV, OWN, 128)
    gi_rows, gf = pl.pallas_call(
        kernel,
        out_shape=(jax.ShapeDtypeStruct(blocks, BF16), jax.ShapeDtypeStruct((2, CHAN_DEV * WIDTH), F32)),
        in_specs=[pl.BlockSpec(memory_space=pltpu.SMEM), anywhere, anywhere, anywhere],
        out_specs=(anywhere, vmem),
        scratch_shapes=[
            pltpu.VMEM((TB, WIDTH), BF16),
            pltpu.VMEM((TB, WIDTH), BF16),
            pltpu.VMEM((2, CHAN_DEV * WIDTH), F32),
            pltpu.VMEM(blocks, BF16),
            pltpu.VMEM(blocks, BF16),
            pltpu.VMEM(blocks, BF16),
            pltpu.VMEM(blocks, BF16),
            pltpu.VMEM(blocks, BF16),
            pltpu.VMEM((CHAN_DEV, 2, WIDTH), F32),
            pltpu.VMEM((8, WIDTH), F32),
            pltpu.VMEM((SEQ_DEV, 128), F32),
            pltpu.VMEM((SEQ_DEV, 128), F32),
            pltpu.VMEM((ROWS + SMAX * OWN, 128), F32),
            pltpu.VMEM((ROWS, 128), F32),
            pltpu.VMEM((ROWS, 128), F32),
            pltpu.VMEM((OWN, 2 * TB, SPAN), BF16),
            pltpu.VMEM((OWN, SEQ_DEV, SPAN), BF16),
            pltpu.VMEM((OWN, LAGS), F32),
            pltpu.VMEM((SMAX, OWN * 8, TB), F32),
            pltpu.VMEM((512, LAGS), BF16),
            pltpu.VMEM((SEQ_DEV, 128), F32),
            pltpu.VMEM((SEQ_DEV, 128), F32),
            pltpu.VMEM((CHAN_DEV, 2, WIDTH), F32),
            pltpu.VMEM((CHAN_DEV, 2, WIDTH), F32),
            pltpu.SemaphoreType.DMA((3,)),
            pltpu.SemaphoreType.DMA((7,)),
            pltpu.SemaphoreType.DMA((7,)),
            pltpu.SemaphoreType.DMA,
        ],
        compiler_params=pltpu.CompilerParams(collective_id=0, has_side_effects=True, vmem_limit_bytes=48 * 2**20),
    )(supports, grads, inputs, filter_taps)
    return pl.pallas_call(
        finish,
        out_shape=(jax.ShapeDtypeStruct((TB, WIDTH), BF16), jax.ShapeDtypeStruct((2, CHAN_DEV * WIDTH), F32)),
        in_specs=[vmem, vmem],
        out_specs=(vmem, vmem),
    )(gi_rows.reshape(ROWS, 128), gf)


def solution(mesh):
    in_specs = (P("seq", "chan"), P("seq", "chan"), P(("seq", "chan"), None), P())
    out_specs = (P("seq", "chan"), P(("seq", "chan"), None))
    return jax.shard_map(body, mesh=mesh, in_specs=in_specs, out_specs=out_specs, check_vma=False)
```

```python
import functools

import jax
import jax.numpy as jnp
from jax import lax
from jax.experimental import pallas as pl
from jax.experimental.pallas import tpu as pltpu
from jax.sharding import PartitionSpec as P

MESH = pl.DeviceIdType.MESH
F32 = jnp.float32
BF16 = jnp.bfloat16
TB = 128
SMAX = 4
SEQ_DEV = 64
CHAN_DEV = 4
WIDTH = 1024
OWN = 16
LAGS = SMAX * TB
SPAN = LAGS + TB
ROWS = SEQ_DEV * OWN
NT = (((1,), (1,)), ((), ()))


def iota(shape, axis):
    return lax.broadcasted_iota(jnp.int32, shape, axis)


def high_low(value):
    high = value.astype(BF16)
    return jnp.concatenate([high, (value - high.astype(F32)).astype(BF16)], axis=0)


def take_all(landed, send_sem, recv_sem, count):
    span = landed.at[pl.ds(0, count)]
    pltpu.make_async_copy(span, span, recv_sem).wait()
    pltpu.make_async_copy(span, span, send_sem).wait()


def each_peer(me, visit):
    y, z, core = me // 16, lax.rem(me // 2, 8), lax.rem(me, 2)

    def ring(step, skip):
        far = 4 + (step + 1) // 2 * (1 - 2 * lax.rem(step, 2))
        for dy in (2, 1, 3, 0):
            chip = lax.rem(y + dy, 4) * 8 + lax.rem(z + far, 8)
            for other in (1, 0):
                if not (skip and dy == 0 and other == 0):
                    visit(chip * 2 + lax.rem(core + other, 2))
        return skip

    def one(step, carry):
        ring(step, False)
        return carry

    lax.fori_loop(0, 7, one, 0)
    ring(jnp.int32(7), True)


def spread(source, landed, send_sem, recv_sem, me):
    def one(to):
        pltpu.make_async_remote_copy(
            source.at[pl.ds(to, 1)], landed.at[pl.ds(me, 1)], send_sem, recv_sem, device_id={"seq": to}, device_id_type=MESH
        ).start()

    each_peer(me, one)


def turn(block_ref, out_ref, backwards):
    mirror = jnp.where(iota((TB, TB), 0) + iota((TB, TB), 1) == TB - 1, 1.0, 0.0).astype(BF16)
    for tile in range(WIDTH // 128):
        flipped = block_ref[:, tile * 128 : (tile + 1) * 128].astype(F32).T.astype(BF16)
        if backwards:
            flipped = jnp.dot(flipped, mirror, preferred_element_type=F32).astype(BF16)
        out_ref[tile * 8 : (tile + 1) * 8] = flipped.reshape(8, OWN, 128)


def kernel(
    supports_far, grads, inputs, taps, gi_out, gf_out,
    supports,
    g_here, x_here, t_here, g_send, x_send, g_land, x_land, gi_send,
    tap_send, tap_land, t_rows, row_send, row_land, g_wide, x_wide, gi_wide, toeplitz, windows, tap_lines, partial,
    order, back_send, back_land, last_send,
    in_sem, send_sem, recv_sem, keep_sem,
):
    me, chan = lax.axis_index("seq"), lax.axis_index("chan")
    phase = lax.rem(me, 8)
    load_g = pltpu.make_async_copy(grads, g_here, in_sem.at[0])
    load_t = pltpu.make_async_copy(taps, t_here, in_sem.at[1])
    load_x = pltpu.make_async_copy(inputs, x_here, in_sem.at[2])
    barrier = pltpu.get_barrier_semaphore()

    def greet(to):
        pl.semaphore_signal(barrier, inc=1, device_id={"seq": to}, device_id_type=MESH)

    each_peer(me, greet)
    for step in (2, 1, 3):
        pl.semaphore_signal(barrier, inc=1, device_id={"chan": lax.rem(chan + step, CHAN_DEV)}, device_id_type=MESH)
    load_s = pltpu.make_async_copy(supports_far, supports, in_sem.at[3])
    load_t.start()
    load_g.start()
    load_s.start()
    load_x.start()

    lane_group, sublane = iota((8, 128), 1) // 16, iota((8, 128), 0)
    load_t.wait()
    for x in range(CHAN_DEV):
        t_rows[2 * x : 2 * x + 2, :] = t_here[:, x * WIDTH : (x + 1) * WIDTH]
    for tile in range(8):
        block = t_rows[:, tile * 128 : (tile + 1) * 128]
        skewed = block
        for r in range(1, 8):
            skewed = jnp.where(sublane == r, pltpu.roll(block, 128 - 16 * r, axis=1), skewed)
        moved = skewed
        for k in range(1, 8):
            moved = jnp.where(lane_group == k, pltpu.roll(skewed, k, axis=0), moved)
        row_send[tile * 8 : (tile + 1) * 8, :] = moved
    row_land[pl.ds(me, 1), :] = row_send[pl.ds(me, 1), :]
    load_g.wait()
    turn(g_here, g_send, False)
    g_land[me] = g_send[me]
    load_x.wait()
    turn(x_here, x_send, True)
    x_land[me] = x_send[me]
    row = iota((512, 1), 0)
    lag_of = (row % 64) * 8 + row // 64
    order[...] = jnp.where(iota((512, LAGS), 1) == lag_of, 1.0, 0.0).astype(BF16)
    g_wide[ROWS:, :] = jnp.zeros((SMAX * OWN, 128), F32)
    load_s.wait()
    own_lags = TB * supports[chan * (WIDTH // 128) + me // 8]
    pl.semaphore_wait(barrier, SEQ_DEV - 1 + CHAN_DEV - 1)

    spread(row_send, row_land, send_sem.at[2], recv_sem.at[2], me)
    spread(g_send, g_land, send_sem.at[1], recv_sem.at[1], me)
    spread(x_send, x_land, send_sem.at[3], recv_sem.at[3], me)
    take_all(row_land, send_sem.at[2], recv_sem.at[2], SEQ_DEV - 1)
    landed = pltpu.roll(row_land[...], lax.rem(8 - phase, 8) * 16, axis=1)
    flipped = jnp.concatenate([landed, pltpu.roll(landed, 16, axis=1)], axis=0).T
    for x in range(CHAN_DEV):
        at = (8 - 2 * x) % 8 * 16
        tap_send[x] = flipped[at : at + 16]
    for step in (2, 1, 3):
        to = lax.rem(chan + step, CHAN_DEV)
        pltpu.make_async_remote_copy(
            tap_send.at[to], tap_land.at[chan], send_sem.at[0], recv_sem.at[0], device_id={"chan": to}, device_id_type=MESH
        ).start()
    tap_land[chan] = tap_send[chan]
    take_all(tap_land, send_sem.at[0], recv_sem.at[0], CHAN_DEV - 1)
    placed = jnp.concatenate([tap_land[x] for x in range(CHAN_DEV)], axis=1)
    both = jnp.dot(high_low(placed), order[...], preferred_element_type=F32)
    tap_lines[...] = jnp.where(iota((OWN, LAGS), 1) < own_lags, both[:OWN] + both[OWN:], 0.0)

    below = iota((TB, TB), 1) >= iota((TB, TB), 0)

    def build(c, carry):
        line = tap_lines[pl.ds(c, 1), :]
        before = jnp.zeros((TB, TB), F32)
        for j in range(SMAX + 1):
            if j < SMAX:
                now = jnp.broadcast_to(line[:, j * TB : (j + 1) * TB], (TB, TB))
                now = pltpu.roll(now, 0, axis=1, stride=1, stride_axis=0)
            else:
                now = jnp.zeros((TB, TB), F32)
            toeplitz[c, :, j * TB : (j + 1) * TB] = high_low(jnp.where(below, now, before))
            before = now
        return carry

    lax.fori_loop(0, OWN, build, 0, unroll=16)

    take_all(g_land, send_sem.at[1], recv_sem.at[1], SEQ_DEV - 1)
    g_wide[0:ROWS, :] = g_land[...].reshape(ROWS, 128).astype(F32)

    def signal_back(c, carry):
        for j in range(SMAX + 1):
            windows[c, :, j * TB : (j + 1) * TB] = g_wide[pl.ds(j * OWN + c, SEQ_DEV, stride=OWN), :].astype(BF16)
        both = lax.dot_general(windows[c], toeplitz[c], NT, preferred_element_type=F32)
        gi_wide[pl.ds(c, SEQ_DEV, stride=OWN), :] = both[:, :TB] + both[:, TB:]
        return carry

    lax.fori_loop(0, OWN, signal_back, 0, unroll=16)
    gi_send[...] = gi_wide[...].astype(BF16).reshape(SEQ_DEV, OWN, 128)
    spread(gi_send, gi_out, send_sem.at[4], recv_sem.at[4], me)
    keep = pltpu.make_async_copy(gi_send.at[pl.ds(me, 1)], gi_out.at[pl.ds(me, 1)], keep_sem.at[0])
    keep.start()

    take_all(x_land, send_sem.at[3], recv_sem.at[3], SEQ_DEV - 1)
    x_wide[...] = x_land[...].reshape(ROWS, 128).astype(F32)
    inside = iota((TB, TB), 1) <= iota((TB, TB), 0)

    def lag_sums(c, carry):
        signal = x_wide[pl.ds(c, SEQ_DEV, stride=OWN), :].T.astype(BF16)
        after = None
        for j in range(SMAX, -1, -1):
            product = jnp.dot(signal, windows[c, :, j * TB : (j + 1) * TB], preferred_element_type=F32)
            now = pltpu.roll(product, 1, axis=1, stride=1, stride_axis=0)
            if j < SMAX:
                lined = jnp.where(inside, now, after)
                partial[j, pl.ds(c * 8, 8), :] = jnp.sum(lined.reshape(TB // 8, 8, TB), axis=0)
            after = now
        return carry

    lax.fori_loop(0, OWN, lag_sums, 0, unroll=16)
    blocks = []
    for j in range(SMAX):
        added = partial[j, pl.ds(0, OWN, stride=8), :]
        for q in range(1, 8):
            added = added + partial[j, pl.ds(q, OWN, stride=8), :]
        blocks.append(added)
    sums = jnp.concatenate(blocks, axis=1)
    sums = jnp.where(iota((OWN, LAGS), 1) < own_lags, sums, 0.0)
    both = lax.dot_general(high_low(sums), order[...], NT, preferred_element_type=F32)
    placed = both[:OWN] + both[OWN:]
    stacked = []
    for p in range(8):
        x = (8 - p) % 8 // 2
        stacked.append(placed[:, x * 128 : (x + 1) * 128] if p % 2 == 0 else jnp.zeros((OWN, 128), F32))
    flipped = jnp.concatenate(stacked, axis=0).T
    back = flipped[:64] + pltpu.roll(flipped[64:], 112, axis=1)
    back_send[...] = pltpu.roll(back, phase * 16, axis=1)
    spread(back_send, back_land, send_sem.at[5], recv_sem.at[5], me)
    back_land[pl.ds(me, 1), :] = back_send[pl.ds(me, 1), :]
    take_all(back_land, send_sem.at[5], recv_sem.at[5], SEQ_DEV - 1)
    for tile in range(8):
        block = back_land[tile * 8 : (tile + 1) * 8, :]
        moved = block
        for k in range(1, 8):
            moved = jnp.where(lane_group == k, pltpu.roll(block, 8 - k, axis=0), moved)
        t_rows[:, tile * 128 : (tile + 1) * 128] = pltpu.roll(moved, 0, axis=1, stride=16, stride_axis=0)
    for x in range(CHAN_DEV):
        last_send[x] = t_rows[2 * x : 2 * x + 2, :]
    for step in (2, 1, 3):
        to = lax.rem(chan + step, CHAN_DEV)
        pltpu.make_async_remote_copy(
            last_send.at[to], gf_out.at[chan], send_sem.at[6], recv_sem.at[6], device_id={"chan": to}, device_id_type=MESH
        ).start()
    keep_f = pltpu.make_async_copy(last_send.at[pl.ds(chan, 1)], gf_out.at[pl.ds(chan, 1)], keep_sem.at[1])
    keep_f.start()
    take_all(gf_out, send_sem.at[6], recv_sem.at[6], CHAN_DEV - 1)
    keep_f.wait()
    keep.wait()
    take_all(gi_out, send_sem.at[4], recv_sem.at[4], SEQ_DEV - 1)


def finish(gi_rows, gf_here, gi, gf):
    for tile in range(WIDTH // 128):
        lanes = slice(tile * 128, (tile + 1) * 128)
        gi[:, lanes] = gi_rows[lanes, :].astype(F32).T.astype(BF16)
    for x in range(CHAN_DEV):
        gf[:, x * WIDTH : (x + 1) * WIDTH] = gf_here[x]


def body(inputs, grads, filter_taps, supports):
    vmem = pl.BlockSpec(memory_space=pltpu.VMEM)
    anywhere = pl.BlockSpec(memory_space=pl.ANY)
    blocks = (SEQ_DEV, OWN, 128)
    gi_rows, gf = pl.pallas_call(
        kernel,
        out_shape=(jax.ShapeDtypeStruct(blocks, BF16), jax.ShapeDtypeStruct((CHAN_DEV, 2, WIDTH), F32)),
        in_specs=[anywhere] * 4,
        out_specs=(anywhere, anywhere),
        scratch_shapes=[
            pltpu.SMEM((32,), jnp.int32),
            pltpu.VMEM((TB, WIDTH), BF16),
            pltpu.VMEM((TB, WIDTH), BF16),
            pltpu.VMEM((2, CHAN_DEV * WIDTH), F32),
            pltpu.VMEM(blocks, BF16),
            pltpu.VMEM(blocks, BF16),
            pltpu.VMEM(blocks, BF16),
            pltpu.VMEM(blocks, BF16),
            pltpu.VMEM(blocks, BF16),
            pltpu.VMEM((CHAN_DEV, OWN, 128), F32),
            pltpu.VMEM((CHAN_DEV, OWN, 128), F32),
            pltpu.VMEM((8, WIDTH), F32),
            pltpu.VMEM((SEQ_DEV, 128), F32),
            pltpu.VMEM((SEQ_DEV, 128), F32),
            pltpu.VMEM((ROWS + SMAX * OWN, 128), F32),
            pltpu.VMEM((ROWS, 128), F32),
            pltpu.VMEM((ROWS, 128), F32),
            pltpu.VMEM((OWN, 2 * TB, SPAN), BF16),
            pltpu.VMEM((OWN, SEQ_DEV, SPAN), BF16),
            pltpu.VMEM((OWN, LAGS), F32),
            pltpu.VMEM((SMAX, OWN * 8, TB), F32),
            pltpu.VMEM((512, LAGS), BF16),
            pltpu.VMEM((SEQ_DEV, 128), F32),
            pltpu.VMEM((SEQ_DEV, 128), F32),
            pltpu.VMEM((CHAN_DEV, 2, WIDTH), F32),
            pltpu.SemaphoreType.DMA((4,)),
            pltpu.SemaphoreType.DMA((7,)),
            pltpu.SemaphoreType.DMA((7,)),
            pltpu.SemaphoreType.DMA((2,)),
        ],
        compiler_params=pltpu.CompilerParams(collective_id=0, has_side_effects=True, vmem_limit_bytes=62 * 2**20),
    )(supports, grads, inputs, filter_taps)
    return pl.pallas_call(
        finish,
        out_shape=(jax.ShapeDtypeStruct((TB, WIDTH), BF16), jax.ShapeDtypeStruct((2, CHAN_DEV * WIDTH), F32)),
        in_specs=[vmem, vmem],
        out_specs=(vmem, vmem),
    )(gi_rows.reshape(ROWS, 128), gf)


def solution(mesh):
    in_specs = (P("seq", "chan"), P("seq", "chan"), P(("seq", "chan"), None), P())
    out_specs = (P("seq", "chan"), P(("seq", "chan"), None))
    return jax.shard_map(body, mesh=mesh, in_specs=in_specs, out_specs=out_specs, check_vma=False)
```

```python
import functools

import jax
import jax.numpy as jnp
from jax import lax
from jax.experimental import pallas as pl
from jax.experimental.pallas import tpu as pltpu
from jax.sharding import PartitionSpec as P

MESH = pl.DeviceIdType.MESH
F32 = jnp.float32
BF16 = jnp.bfloat16
TB = 128
SMAX = 4
SEQ_DEV = 64
CHAN_DEV = 4
WIDTH = 1024
OWN = 16
LAGS = SMAX * TB
SPAN = LAGS + TB
ROWS = SEQ_DEV * OWN
NT = (((1,), (1,)), ((), ()))


def iota(shape, axis):
    return lax.broadcasted_iota(jnp.int32, shape, axis)


def high_low(value):
    high = value.astype(BF16)
    return jnp.concatenate([high, (value - high.astype(F32)).astype(BF16)], axis=0)


def take_all(landed, send_sem, recv_sem, count):
    span = landed.at[pl.ds(0, count)]
    pltpu.make_async_copy(span, span, recv_sem).wait()
    pltpu.make_async_copy(span, span, send_sem).wait()


def each_peer(me, visit):
    y, z, core = me // 16, lax.rem(me // 2, 8), lax.rem(me, 2)

    def ring(step, skip):
        far = 4 + (step + 1) // 2 * (1 - 2 * lax.rem(step, 2))
        for dy in (2, 1, 3, 0):
            chip = lax.rem(y + dy, 4) * 8 + lax.rem(z + far, 8)
            for other in (1, 0):
                if not (skip and dy == 0 and other == 0):
                    visit(chip * 2 + lax.rem(core + other, 2))
        return skip

    def one(step, carry):
        ring(step, False)
        return carry

    lax.fori_loop(0, 7, one, 0)
    ring(jnp.int32(7), True)


def spread(source, landed, send_sem, recv_sem, me):
    def one(to):
        pltpu.make_async_remote_copy(
            source.at[pl.ds(to, 1)], landed.at[pl.ds(me, 1)], send_sem, recv_sem, device_id={"seq": to}, device_id_type=MESH
        ).start()

    each_peer(me, one)


def turn(block_ref, out_ref, backwards):
    mirror = jnp.where(iota((TB, TB), 0) + iota((TB, TB), 1) == TB - 1, 1.0, 0.0).astype(BF16)
    for tile in range(WIDTH // 128):
        flipped = block_ref[:, tile * 128 : (tile + 1) * 128].astype(F32).T.astype(BF16)
        if backwards:
            flipped = jnp.dot(flipped, mirror, preferred_element_type=F32).astype(BF16)
        out_ref[tile * 8 : (tile + 1) * 8] = flipped.reshape(8, OWN, 128)


def kernel(
    supports_far, grads, inputs, taps, gi_out, gf_out,
    supports,
    g_here, x_here, t_here, g_send, x_send, g_land, x_land, gi_send,
    tap_send, tap_land, t_rows, row_send, row_land, g_wide, x_wide, gi_wide, toeplitz, windows, tap_lines, partial,
    order, back_send, gi_land, gi_here,
    in_sem, send_sem, recv_sem, keep_sem,
):
    me, chan = lax.axis_index("seq"), lax.axis_index("chan")
    phase = lax.rem(me, 8)
    load_g = pltpu.make_async_copy(grads, g_here, in_sem.at[0])
    load_t = pltpu.make_async_copy(taps, t_here, in_sem.at[1])
    load_x = pltpu.make_async_copy(inputs, x_here, in_sem.at[2])
    barrier = pltpu.get_barrier_semaphore()

    def greet(to):
        pl.semaphore_signal(barrier, inc=1, device_id={"seq": to}, device_id_type=MESH)

    each_peer(me, greet)
    for step in (2, 1, 3):
        pl.semaphore_signal(barrier, inc=1, device_id={"chan": lax.rem(chan + step, CHAN_DEV)}, device_id_type=MESH)
    load_s = pltpu.make_async_copy(supports_far, supports, in_sem.at[3])
    load_t.start()
    load_g.start()
    load_s.start()
    load_x.start()

    lane_group, sublane = iota((8, 128), 1) // 16, iota((8, 128), 0)
    load_t.wait()
    for x in range(CHAN_DEV):
        t_rows[2 * x : 2 * x + 2, :] = t_here[:, x * WIDTH : (x + 1) * WIDTH]
    for tile in range(8):
        block = t_rows[:, tile * 128 : (tile + 1) * 128]
        skewed = block
        for r in range(1, 8):
            skewed = jnp.where(sublane == r, pltpu.roll(block, 128 - 16 * r, axis=1), skewed)
        moved = skewed
        for k in range(1, 8):
            moved = jnp.where(lane_group == k, pltpu.roll(skewed, k, axis=0), moved)
        row_send[tile * 8 : (tile + 1) * 8, :] = moved
    row_land[pl.ds(me, 1), :] = row_send[pl.ds(me, 1), :]
    load_g.wait()
    turn(g_here, g_send, False)
    g_land[me] = g_send[me]
    load_x.wait()
    turn(x_here, x_send, True)
    x_land[me] = x_send[me]
    row = iota((512, 1), 0)
    lag_of = (row % 64) * 8 + row // 64
    order[...] = jnp.where(iota((512, LAGS), 1) == lag_of, 1.0, 0.0).astype(BF16)
    g_wide[ROWS:, :] = jnp.zeros((SMAX * OWN, 128), F32)
    load_s.wait()
    own_lags = TB * supports[chan * (WIDTH // 128) + me // 8]
    pl.semaphore_wait(barrier, SEQ_DEV - 1 + CHAN_DEV - 1)

    spread(row_send, row_land, send_sem.at[2], recv_sem.at[2], me)
    spread(g_send, g_land, send_sem.at[1], recv_sem.at[1], me)
    spread(x_send, x_land, send_sem.at[3], recv_sem.at[3], me)
    take_all(row_land, send_sem.at[2], recv_sem.at[2], SEQ_DEV - 1)
    landed = pltpu.roll(row_land[...], lax.rem(8 - phase, 8) * 16, axis=1)
    flipped = jnp.concatenate([landed, pltpu.roll(landed, 16, axis=1)], axis=0).T
    for x in range(CHAN_DEV):
        at = (8 - 2 * x) % 8 * 16
        tap_send[x] = flipped[at : at + 16]
    for step in (2, 1, 3):
        to = lax.rem(chan + step, CHAN_DEV)
        pltpu.make_async_remote_copy(
            tap_send.at[to], tap_land.at[chan], send_sem.at[0], recv_sem.at[0], device_id={"chan": to}, device_id_type=MESH
        ).start()
    tap_land[chan] = tap_send[chan]
    take_all(tap_land, send_sem.at[0], recv_sem.at[0], CHAN_DEV - 1)
    placed = jnp.concatenate([tap_land[x] for x in range(CHAN_DEV)], axis=1)
    both = jnp.dot(high_low(placed), order[...], preferred_element_type=F32)
    tap_lines[...] = jnp.where(iota((OWN, LAGS), 1) < own_lags, both[:OWN] + both[OWN:], 0.0)

    below = iota((TB, TB), 1) >= iota((TB, TB), 0)

    def build(c, carry):
        line = tap_lines[pl.ds(c, 1), :]
        before = jnp.zeros((TB, TB), F32)
        for j in range(SMAX + 1):
            if j < SMAX:
                now = jnp.broadcast_to(line[:, j * TB : (j + 1) * TB], (TB, TB))
                now = pltpu.roll(now, 0, axis=1, stride=1, stride_axis=0)
            else:
                now = jnp.zeros((TB, TB), F32)
            toeplitz[c, :, j * TB : (j + 1) * TB] = high_low(jnp.where(below, now, before))
            before = now
        return carry

    lax.fori_loop(0, OWN, build, 0, unroll=16)

    take_all(g_land, send_sem.at[1], recv_sem.at[1], SEQ_DEV - 1)
    g_wide[0:ROWS, :] = g_land[...].reshape(ROWS, 128).astype(F32)

    def signal_back(c, carry):
        for j in range(SMAX + 1):
            windows[c, :, j * TB : (j + 1) * TB] = g_wide[pl.ds(j * OWN + c, SEQ_DEV, stride=OWN), :].astype(BF16)
        both = lax.dot_general(windows[c], toeplitz[c], NT, preferred_element_type=F32)
        gi_wide[pl.ds(c, SEQ_DEV, stride=OWN), :] = both[:, :TB] + both[:, TB:]
        return carry

    lax.fori_loop(0, OWN, signal_back, 0, unroll=16)
    gi_send[...] = gi_wide[...].astype(BF16).reshape(SEQ_DEV, OWN, 128)
    spread(gi_send, gi_land, send_sem.at[4], recv_sem.at[4], me)
    gi_land[me] = gi_send[me]

    take_all(x_land, send_sem.at[3], recv_sem.at[3], SEQ_DEV - 1)
    x_wide[...] = x_land[...].reshape(ROWS, 128).astype(F32)
    inside = iota((TB, TB), 1) <= iota((TB, TB), 0)

    def lag_sums(c, carry):
        signal = x_wide[pl.ds(c, SEQ_DEV, stride=OWN), :].T.astype(BF16)
        after = None
        for j in range(SMAX, -1, -1):
            product = jnp.dot(signal, windows[c, :, j * TB : (j + 1) * TB], preferred_element_type=F32)
            now = pltpu.roll(product, 1, axis=1, stride=1, stride_axis=0)
            if j < SMAX:
                lined = jnp.where(inside, now, after)
                partial[j, pl.ds(c * 8, 8), :] = jnp.sum(lined.reshape(TB // 8, 8, TB), axis=0)
            after = now
        return carry

    lax.fori_loop(0, OWN, lag_sums, 0, unroll=16)
    blocks = []
    for j in range(SMAX):
        added = partial[j, pl.ds(0, OWN, stride=8), :]
        for q in range(1, 8):
            added = added + partial[j, pl.ds(q, OWN, stride=8), :]
        blocks.append(added)
    sums = jnp.concatenate(blocks, axis=1)
    sums = jnp.where(iota((OWN, LAGS), 1) < own_lags, sums, 0.0)
    both = lax.dot_general(high_low(sums), order[...], NT, preferred_element_type=F32)
    placed = both[:OWN] + both[OWN:]
    stacked = []
    for p in range(8):
        x = (8 - p) % 8 // 2
        stacked.append(placed[:, x * 128 : (x + 1) * 128] if p % 2 == 0 else jnp.zeros((OWN, 128), F32))
    flipped = jnp.concatenate(stacked, axis=0).T
    back = flipped[:64] + pltpu.roll(flipped[64:], 112, axis=1)
    back_send[...] = pltpu.roll(back, phase * 16, axis=1)
    def to_owners(to):
        for step in (2, 1, 3, 0):
            other = lax.rem(chan + step, CHAN_DEV)
            pltpu.make_async_remote_copy(
                back_send.at[pl.ds(to, 1)], gf_out.at[pl.ds(chan * SEQ_DEV + me, 1)], send_sem.at[5], recv_sem.at[5],
                device_id={"seq": to, "chan": other}, device_id_type=MESH,
            ).start()

    each_peer(me, to_owners)
    for step in (2, 1, 3):
        other = lax.rem(chan + step, CHAN_DEV)
        pltpu.make_async_remote_copy(
            back_send.at[pl.ds(me, 1)], gf_out.at[pl.ds(chan * SEQ_DEV + me, 1)], send_sem.at[5], recv_sem.at[5],
            device_id={"chan": other}, device_id_type=MESH,
        ).start()
    keep = pltpu.make_async_copy(back_send.at[pl.ds(me, 1)], gf_out.at[pl.ds(chan * SEQ_DEV + me, 1)], keep_sem.at[0])
    keep.start()
    take_all(gi_land, send_sem.at[4], recv_sem.at[4], SEQ_DEV - 1)
    for tile in range(WIDTH // 128):
        rows = gi_land[tile * 8 : (tile + 1) * 8].reshape(128, 128)
        gi_here[:, tile * 128 : (tile + 1) * 128] = rows.astype(F32).T.astype(BF16)
    store = pltpu.make_async_copy(gi_here, gi_out, keep_sem.at[1])
    store.start()
    keep.wait()
    take_all(gf_out, send_sem.at[5], recv_sem.at[5], CHAN_DEV * SEQ_DEV - 1)
    store.wait()


def finish(gi_here, gf_rows, gi, gf, gf_here, sem):
    store = pltpu.make_async_copy(gi_here, gi, sem.at[0])
    store.start()
    group = iota((32, 128), 1) // 16
    for half in range(2):
        lag = 2 * lax.axis_index("chan") + half
        line = jnp.zeros((32, 128), F32)
        for a in range(8):
            line = jnp.where(group == ((a + 8 - lag) & 7), gf_rows[pl.ds(a, 32, stride=8), :], line)
        line = pltpu.roll(line, 16 * lag, axis=1)
        for tile in range(32):
            gf_here[half : half + 1, tile * 128 : (tile + 1) * 128] = line[tile : tile + 1, :]
    store_f = pltpu.make_async_copy(gf_here, gf, sem.at[1])
    store_f.start()
    store.wait()
    store_f.wait()


def body(inputs, grads, filter_taps, supports):
    anywhere = pl.BlockSpec(memory_space=pl.ANY)
    blocks = (SEQ_DEV, OWN, 128)
    gi, gf_rows = pl.pallas_call(
        kernel,
        out_shape=(pltpu.VMEM((TB, WIDTH), BF16), pltpu.VMEM((CHAN_DEV * SEQ_DEV, 128), F32)),
        in_specs=[anywhere] * 4,
        out_specs=(anywhere, anywhere),
        scratch_shapes=[
            pltpu.SMEM((32,), jnp.int32),
            pltpu.VMEM((TB, WIDTH), BF16),
            pltpu.VMEM((TB, WIDTH), BF16),
            pltpu.VMEM((2, CHAN_DEV * WIDTH), F32),
            pltpu.VMEM(blocks, BF16),
            pltpu.VMEM(blocks, BF16),
            pltpu.VMEM(blocks, BF16),
            pltpu.VMEM(blocks, BF16),
            pltpu.VMEM(blocks, BF16),
            pltpu.VMEM((CHAN_DEV, OWN, 128), F32),
            pltpu.VMEM((CHAN_DEV, OWN, 128), F32),
            pltpu.VMEM((8, WIDTH), F32),
            pltpu.VMEM((SEQ_DEV, 128), F32),
            pltpu.VMEM((SEQ_DEV, 128), F32),
            pltpu.VMEM((ROWS + SMAX * OWN, 128), F32),
            pltpu.VMEM((ROWS, 128), F32),
            pltpu.VMEM((ROWS, 128), F32),
            pltpu.VMEM((OWN, 2 * TB, SPAN), BF16),
            pltpu.VMEM((OWN, SEQ_DEV, SPAN), BF16),
            pltpu.VMEM((OWN, LAGS), F32),
            pltpu.VMEM((SMAX, OWN * 8, TB), F32),
            pltpu.VMEM((512, LAGS), BF16),
            pltpu.VMEM((SEQ_DEV, 128), F32),
            pltpu.VMEM(blocks, BF16),
            pltpu.VMEM((TB, WIDTH), BF16),
            pltpu.SemaphoreType.DMA((4,)),
            pltpu.SemaphoreType.DMA((6,)),
            pltpu.SemaphoreType.DMA((6,)),
            pltpu.SemaphoreType.DMA((2,)),
        ],
        compiler_params=pltpu.CompilerParams(collective_id=0, has_side_effects=True, vmem_limit_bytes=48 * 2**20),
    )(*(pltpu.with_memory_space_constraint(a, pltpu.HBM) for a in (supports, grads, inputs, filter_taps)))
    return pl.pallas_call(
        finish,
        out_shape=(jax.ShapeDtypeStruct((TB, WIDTH), BF16), jax.ShapeDtypeStruct((2, CHAN_DEV * WIDTH), F32)),
        in_specs=[pl.BlockSpec(memory_space=pltpu.VMEM)] * 2,
        out_specs=(anywhere, anywhere),
        scratch_shapes=[pltpu.VMEM((2, CHAN_DEV * WIDTH), F32), pltpu.SemaphoreType.DMA((2,))],
        compiler_params=pltpu.CompilerParams(vmem_limit_bytes=8 * 2**20),
    )(gi, gf_rows)


def solution(mesh):
    in_specs = (P("seq", "chan"), P("seq", "chan"), P(("seq", "chan"), None), P())
    out_specs = (P("seq", "chan"), P(("seq", "chan"), None))
    return jax.shard_map(body, mesh=mesh, in_specs=in_specs, out_specs=out_specs, check_vma=False)
```

```python
import functools

import jax
import jax.numpy as jnp
from jax import lax
from jax.experimental import pallas as pl
from jax.experimental.pallas import tpu as pltpu
from jax.sharding import PartitionSpec as P

MESH = pl.DeviceIdType.MESH
F32 = jnp.float32
BF16 = jnp.bfloat16
TB = 128
SMAX = 4
SEQ_DEV = 64
CHAN_DEV = 4
WIDTH = 1024
OWN = 16
LAGS = SMAX * TB
SPAN = LAGS + TB
ROWS = SEQ_DEV * OWN
NT = (((1,), (1,)), ((), ()))


def iota(shape, axis):
    return lax.broadcasted_iota(jnp.int32, shape, axis)


def high_low(value):
    high = value.astype(BF16)
    return jnp.concatenate([high, (value - high.astype(F32)).astype(BF16)], axis=0)


def take_all(landed, send_sem, recv_sem, count):
    span = landed.at[pl.ds(0, count)]
    pltpu.make_async_copy(span, span, recv_sem).wait()
    pltpu.make_async_copy(span, span, send_sem).wait()


def each_peer(me, visit):
    y, z, core = me // 16, lax.rem(me // 2, 8), lax.rem(me, 2)

    def ring(step, skip):
        far = 4 + (step + 1) // 2 * (1 - 2 * lax.rem(step, 2))
        for dy in (2, 1, 3, 0):
            chip = lax.rem(y + dy, 4) * 8 + lax.rem(z + far, 8)
            for other in (1, 0):
                if not (skip and dy == 0 and other == 0):
                    visit(chip * 2 + lax.rem(core + other, 2))
        return skip

    def one(step, carry):
        ring(step, False)
        return carry

    lax.fori_loop(0, 7, one, 0)
    ring(jnp.int32(7), True)


def in_order(me, visit):
    def ring(z, carry):
        for y in range(4):
            for core in range(2):
                to = (y * 8 + z) * 2 + core

                @pl.when(to != me)
                def _():
                    visit(to)

        return carry

    lax.fori_loop(0, 8, ring, 0)


def spread(source, landed, send_sem, recv_sem, me):
    def one(to):
        pltpu.make_async_remote_copy(
            source.at[pl.ds(to, 1)], landed.at[pl.ds(me, 1)], send_sem, recv_sem, device_id={"seq": to}, device_id_type=MESH
        ).start()

    each_peer(me, one)


def turn(block_ref, out_ref, backwards):
    mirror = jnp.where(iota((TB, TB), 0) + iota((TB, TB), 1) == TB - 1, 1.0, 0.0).astype(BF16)
    for tile in range(WIDTH // 128):
        flipped = block_ref[:, tile * 128 : (tile + 1) * 128].astype(F32).T.astype(BF16)
        if backwards:
            flipped = jnp.dot(flipped, mirror, preferred_element_type=F32).astype(BF16)
        out_ref[tile * 8 : (tile + 1) * 8] = flipped.reshape(8, OWN, 128)


def kernel(
    supports_far, grads, inputs, taps, gi_out, gf_out,
    supports,
    g_here, x_here, t_here, g_send, x_send, g_land, x_land, gi_send,
    tap_send, tap_land, t_rows, row_send, row_land, g_wide, x_wide, gi_wide, toeplitz, windows, tap_lines, partial,
    order, back_send, gi_land, gi_here,
    in_sem, send_sem, recv_sem, keep_sem,
):
    me, chan = lax.axis_index("seq"), lax.axis_index("chan")
    phase = lax.rem(me, 8)
    load_g = pltpu.make_async_copy(grads, g_here, in_sem.at[0])
    load_t = pltpu.make_async_copy(taps, t_here, in_sem.at[1])
    load_x = pltpu.make_async_copy(inputs, x_here, in_sem.at[2])
    barrier = pltpu.get_barrier_semaphore()

    def greet(to):
        pl.semaphore_signal(barrier, inc=1, device_id={"seq": to}, device_id_type=MESH)

    each_peer(me, greet)
    for step in (2, 1, 3):
        pl.semaphore_signal(barrier, inc=1, device_id={"chan": lax.rem(chan + step, CHAN_DEV)}, device_id_type=MESH)
    load_s = pltpu.make_async_copy(supports_far, supports, in_sem.at[3])
    load_t.start()
    load_g.start()
    load_s.start()
    load_x.start()

    lane_group, sublane = iota((8, 128), 1) // 16, iota((8, 128), 0)
    load_t.wait()
    for x in range(CHAN_DEV):
        t_rows[2 * x : 2 * x + 2, :] = t_here[:, x * WIDTH : (x + 1) * WIDTH]
    for tile in range(8):
        block = t_rows[:, tile * 128 : (tile + 1) * 128]
        skewed = block
        for r in range(1, 8):
            skewed = jnp.where(sublane == r, pltpu.roll(block, 128 - 16 * r, axis=1), skewed)
        moved = skewed
        for k in range(1, 8):
            moved = jnp.where(lane_group == k, pltpu.roll(skewed, k, axis=0), moved)
        row_send[tile * 8 : (tile + 1) * 8, :] = moved
    row_land[pl.ds(me, 1), :] = row_send[pl.ds(me, 1), :]
    load_g.wait()
    turn(g_here, g_send, False)
    g_land[me] = g_send[me]
    load_x.wait()
    turn(x_here, x_send, True)
    x_land[me] = x_send[me]
    pl.semaphore_wait(barrier, SEQ_DEV - 1 + CHAN_DEV - 1)

    spread(row_send, row_land, send_sem.at[2], recv_sem.at[2], me)
    spread(g_send, g_land, send_sem.at[1], recv_sem.at[1], me)
    spread(x_send, x_land, send_sem.at[3], recv_sem.at[3], me)
    row = iota((512, 1), 0)
    lag_of = (row % 64) * 8 + row // 64
    order[...] = jnp.where(iota((512, LAGS), 1) == lag_of, 1.0, 0.0).astype(BF16)
    g_wide[ROWS:, :] = jnp.zeros((SMAX * OWN, 128), F32)
    load_s.wait()
    own_lags = TB * supports[chan * (WIDTH // 128) + me // 8]
    take_all(row_land, send_sem.at[2], recv_sem.at[2], SEQ_DEV - 1)
    landed = pltpu.roll(row_land[...], lax.rem(8 - phase, 8) * 16, axis=1)
    flipped = jnp.concatenate([landed, pltpu.roll(landed, 16, axis=1)], axis=0).T
    for x in range(CHAN_DEV):
        at = (8 - 2 * x) % 8 * 16
        tap_send[x] = flipped[at : at + 16]
    for step in (2, 1, 3):
        to = lax.rem(chan + step, CHAN_DEV)
        pltpu.make_async_remote_copy(
            tap_send.at[to], tap_land.at[chan], send_sem.at[0], recv_sem.at[0], device_id={"chan": to}, device_id_type=MESH
        ).start()
    tap_land[chan] = tap_send[chan]
    take_all(tap_land, send_sem.at[0], recv_sem.at[0], CHAN_DEV - 1)
    placed = jnp.concatenate([tap_land[x] for x in range(CHAN_DEV)], axis=1)
    both = jnp.dot(high_low(placed), order[...], preferred_element_type=F32)
    tap_lines[...] = jnp.where(iota((OWN, LAGS), 1) < own_lags, both[:OWN] + both[OWN:], 0.0)

    below = iota((TB, TB), 1) >= iota((TB, TB), 0)

    def build(c, carry):
        line = tap_lines[pl.ds(c, 1), :]
        before = jnp.zeros((TB, TB), F32)
        for j in range(SMAX + 1):
            if j < SMAX:
                now = jnp.broadcast_to(line[:, j * TB : (j + 1) * TB], (TB, TB))
                now = pltpu.roll(now, 0, axis=1, stride=1, stride_axis=0)
            else:
                now = jnp.zeros((TB, TB), F32)
            toeplitz[c, :, j * TB : (j + 1) * TB] = high_low(jnp.where(below, now, before))
            before = now
        return carry

    lax.fori_loop(0, OWN, build, 0, unroll=16)

    take_all(g_land, send_sem.at[1], recv_sem.at[1], SEQ_DEV - 1)
    g_wide[0:ROWS, :] = g_land[...].reshape(ROWS, 128).astype(F32)

    def signal_back(c, carry):
        for j in range(SMAX + 1):
            windows[c, :, j * TB : (j + 1) * TB] = g_wide[pl.ds(j * OWN + c, SEQ_DEV, stride=OWN), :].astype(BF16)
        both = lax.dot_general(windows[c], toeplitz[c], NT, preferred_element_type=F32)
        gi_wide[pl.ds(c, SEQ_DEV, stride=OWN), :] = both[:, :TB] + both[:, TB:]
        return carry

    lax.fori_loop(0, OWN, signal_back, 0, unroll=16)
    gi_send[...] = gi_wide[...].astype(BF16).reshape(SEQ_DEV, OWN, 128)
    spread(gi_send, gi_land, send_sem.at[4], recv_sem.at[4], me)
    gi_land[me] = gi_send[me]

    take_all(x_land, send_sem.at[3], recv_sem.at[3], SEQ_DEV - 1)
    x_wide[...] = x_land[...].reshape(ROWS, 128).astype(F32)
    inside = iota((TB, TB), 1) <= iota((TB, TB), 0)

    def lag_sums(c, carry):
        signal = x_wide[pl.ds(c, SEQ_DEV, stride=OWN), :].T.astype(BF16)
        after = None
        for j in range(SMAX, -1, -1):
            product = jnp.dot(signal, windows[c, :, j * TB : (j + 1) * TB], preferred_element_type=F32)
            now = pltpu.roll(product, 1, axis=1, stride=1, stride_axis=0)
            if j < SMAX:
                lined = jnp.where(inside, now, after)
                partial[j, pl.ds(c * 8, 8), :] = jnp.sum(lined.reshape(TB // 8, 8, TB), axis=0)
            after = now
        return carry

    lax.fori_loop(0, OWN, lag_sums, 0, unroll=16)
    blocks = []
    for j in range(SMAX):
        added = partial[j, pl.ds(0, OWN, stride=8), :]
        for q in range(1, 8):
            added = added + partial[j, pl.ds(q, OWN, stride=8), :]
        blocks.append(added)
    sums = jnp.concatenate(blocks, axis=1)
    sums = jnp.where(iota((OWN, LAGS), 1) < own_lags, sums, 0.0)
    both = lax.dot_general(high_low(sums), order[...], NT, preferred_element_type=F32)
    placed = both[:OWN] + both[OWN:]
    stacked = []
    for p in range(8):
        x = (8 - p) % 8 // 2
        stacked.append(placed[:, x * 128 : (x + 1) * 128] if p % 2 == 0 else jnp.zeros((OWN, 128), F32))
    flipped = jnp.concatenate(stacked, axis=0).T
    back = flipped[:64] + pltpu.roll(flipped[64:], 112, axis=1)
    back_send[...] = pltpu.roll(back, phase * 16, axis=1)
    def to_owners(to):
        for step in (2, 1, 3, 0):
            other = lax.rem(chan + step, CHAN_DEV)
            pltpu.make_async_remote_copy(
                back_send.at[pl.ds(to, 1)], gf_out.at[pl.ds(chan * SEQ_DEV + me, 1)], send_sem.at[5], recv_sem.at[5],
                device_id={"seq": to, "chan": other}, device_id_type=MESH,
            ).start()

    in_order(me, to_owners)
    for step in (2, 1, 3):
        other = lax.rem(chan + step, CHAN_DEV)
        pltpu.make_async_remote_copy(
            back_send.at[pl.ds(me, 1)], gf_out.at[pl.ds(chan * SEQ_DEV + me, 1)], send_sem.at[5], recv_sem.at[5],
            device_id={"chan": other}, device_id_type=MESH,
        ).start()
    keep = pltpu.make_async_copy(back_send.at[pl.ds(me, 1)], gf_out.at[pl.ds(chan * SEQ_DEV + me, 1)], keep_sem.at[0])
    keep.start()
    take_all(gi_land, send_sem.at[4], recv_sem.at[4], SEQ_DEV - 1)
    for tile in range(WIDTH // 128):
        rows = gi_land[tile * 8 : (tile + 1) * 8].reshape(128, 128)
        gi_here[:, tile * 128 : (tile + 1) * 128] = rows.astype(F32).T.astype(BF16)
    store = pltpu.make_async_copy(gi_here, gi_out, keep_sem.at[1])
    store.start()
    keep.wait()
    take_all(gf_out, send_sem.at[5], recv_sem.at[5], CHAN_DEV * SEQ_DEV - 1)
    store.wait()


def finish(gi_here, gf_rows, gi, gf, gf_here, sem):
    store = pltpu.make_async_copy(gi_here, gi, sem.at[0])
    store.start()
    group = iota((32, 128), 1) // 16
    for half in range(2):
        lag = 2 * lax.axis_index("chan") + half
        line = jnp.zeros((32, 128), F32)
        for a in range(8):
            line = jnp.where(group == ((a + 8 - lag) & 7), gf_rows[pl.ds(a, 32, stride=8), :], line)
        line = pltpu.roll(line, 16 * lag, axis=1)
        for tile in range(32):
            gf_here[half : half + 1, tile * 128 : (tile + 1) * 128] = line[tile : tile + 1, :]
    store_f = pltpu.make_async_copy(gf_here, gf, sem.at[1])
    store_f.start()
    store.wait()
    store_f.wait()


def body(inputs, grads, filter_taps, supports):
    anywhere = pl.BlockSpec(memory_space=pl.ANY)
    blocks = (SEQ_DEV, OWN, 128)
    gi, gf_rows = pl.pallas_call(
        kernel,
        out_shape=(pltpu.VMEM((TB, WIDTH), BF16), pltpu.VMEM((CHAN_DEV * SEQ_DEV, 128), F32)),
        in_specs=[anywhere] * 4,
        out_specs=(anywhere, anywhere),
        scratch_shapes=[
            pltpu.SMEM((32,), jnp.int32),
            pltpu.VMEM((TB, WIDTH), BF16),
            pltpu.VMEM((TB, WIDTH), BF16),
            pltpu.VMEM((2, CHAN_DEV * WIDTH), F32),
            pltpu.VMEM(blocks, BF16),
            pltpu.VMEM(blocks, BF16),
            pltpu.VMEM(blocks, BF16),
            pltpu.VMEM(blocks, BF16),
            pltpu.VMEM(blocks, BF16),
            pltpu.VMEM((CHAN_DEV, OWN, 128), F32),
            pltpu.VMEM((CHAN_DEV, OWN, 128), F32),
            pltpu.VMEM((8, WIDTH), F32),
            pltpu.VMEM((SEQ_DEV, 128), F32),
            pltpu.VMEM((SEQ_DEV, 128), F32),
            pltpu.VMEM((ROWS + SMAX * OWN, 128), F32),
            pltpu.VMEM((ROWS, 128), F32),
            pltpu.VMEM((ROWS, 128), F32),
            pltpu.VMEM((OWN, 2 * TB, SPAN), BF16),
            pltpu.VMEM((OWN, SEQ_DEV, SPAN), BF16),
            pltpu.VMEM((OWN, LAGS), F32),
            pltpu.VMEM((SMAX, OWN * 8, TB), F32),
            pltpu.VMEM((512, LAGS), BF16),
            pltpu.VMEM((SEQ_DEV, 128), F32),
            pltpu.VMEM(blocks, BF16),
            pltpu.VMEM((TB, WIDTH), BF16),
            pltpu.SemaphoreType.DMA((4,)),
            pltpu.SemaphoreType.DMA((6,)),
            pltpu.SemaphoreType.DMA((6,)),
            pltpu.SemaphoreType.DMA((2,)),
        ],
        compiler_params=pltpu.CompilerParams(collective_id=0, has_side_effects=True, vmem_limit_bytes=48 * 2**20),
    )(*(pltpu.with_memory_space_constraint(a, pltpu.HBM) for a in (supports, grads, inputs, filter_taps)))
    return pl.pallas_call(
        finish,
        out_shape=(jax.ShapeDtypeStruct((TB, WIDTH), BF16), jax.ShapeDtypeStruct((2, CHAN_DEV * WIDTH), F32)),
        in_specs=[pl.BlockSpec(memory_space=pltpu.VMEM)] * 2,
        out_specs=(anywhere, anywhere),
        scratch_shapes=[pltpu.VMEM((2, CHAN_DEV * WIDTH), F32), pltpu.SemaphoreType.DMA((2,))],
        compiler_params=pltpu.CompilerParams(vmem_limit_bytes=8 * 2**20),
    )(gi, gf_rows)


def solution(mesh):
    in_specs = (P("seq", "chan"), P("seq", "chan"), P(("seq", "chan"), None), P())
    out_specs = (P("seq", "chan"), P(("seq", "chan"), None))
    return jax.shard_map(body, mesh=mesh, in_specs=in_specs, out_specs=out_specs, check_vma=False)
```

```python
import functools

import jax
import jax.numpy as jnp
from jax import lax
from jax.experimental import pallas as pl
from jax.experimental.pallas import tpu as pltpu
from jax.sharding import PartitionSpec as P

MESH = pl.DeviceIdType.MESH
F32 = jnp.float32
BF16 = jnp.bfloat16
TB = 128
SMAX = 4
SEQ_DEV = 64
CHAN_DEV = 4
WIDTH = 1024
OWN = 16
LAGS = SMAX * TB
SPAN = LAGS + TB
ROWS = SEQ_DEV * OWN
NT = (((1,), (1,)), ((), ()))


def iota(shape, axis):
    return lax.broadcasted_iota(jnp.int32, shape, axis)


def high_low(value):
    high = value.astype(BF16)
    return jnp.concatenate([high, (value - high.astype(F32)).astype(BF16)], axis=0)


def take_all(landed, send_sem, recv_sem, count):
    span = landed.at[pl.ds(0, count)]
    pltpu.make_async_copy(span, span, recv_sem).wait()
    pltpu.make_async_copy(span, span, send_sem).wait()


def each_peer(me, visit):
    y, z, core = me // 16, lax.rem(me // 2, 8), lax.rem(me, 2)

    def ring(step, skip):
        far = 4 + (step + 1) // 2 * (1 - 2 * lax.rem(step, 2))
        for dy in (2, 1, 3, 0):
            chip = lax.rem(y + dy, 4) * 8 + lax.rem(z + far, 8)
            for other in (1, 0):
                if not (skip and dy == 0 and other == 0):
                    visit(chip * 2 + lax.rem(core + other, 2))
        return skip

    def one(step, carry):
        ring(step, False)
        return carry

    lax.fori_loop(0, 7, one, 0)
    ring(jnp.int32(7), True)


def in_order(me, visit):
    y, here, core = me // 16, lax.rem(me // 2, 8), lax.rem(me, 2)

    def ring(z, carry):
        for dy in (2, 1, 3, 0):
            chip = lax.rem(y + dy, 4) * 8 + z
            visit(chip * 2 + 1 - core)
            if dy:
                visit(chip * 2 + core)
            else:

                @pl.when(z != here)
                def _():
                    visit(chip * 2 + core)

        return carry

    lax.fori_loop(0, 8, ring, 0)


def spread(source, landed, send_sem, recv_sem, me):
    def one(to):
        pltpu.make_async_remote_copy(
            source.at[pl.ds(to, 1)], landed.at[pl.ds(me, 1)], send_sem, recv_sem, device_id={"seq": to}, device_id_type=MESH
        ).start()

    each_peer(me, one)


def turn(block_ref, out_ref, backwards):
    mirror = jnp.where(iota((TB, TB), 0) + iota((TB, TB), 1) == TB - 1, 1.0, 0.0).astype(BF16)
    for tile in range(WIDTH // 128):
        flipped = block_ref[:, tile * 128 : (tile + 1) * 128].astype(F32).T.astype(BF16)
        if backwards:
            flipped = jnp.dot(flipped, mirror, preferred_element_type=F32).astype(BF16)
        out_ref[tile * 8 : (tile + 1) * 8] = flipped.reshape(8, OWN, 128)


def kernel(
    supports_far, grads, inputs, taps, gi_out, gf_out,
    supports,
    g_here, x_here, t_here, g_send, x_send, g_land, x_land, gi_send,
    tap_send, tap_land, t_rows, row_send, row_land, g_wide, x_wide, gi_wide, toeplitz, windows, tap_lines, partial,
    order, back_send, gi_land, gi_here,
    in_sem, send_sem, recv_sem, keep_sem,
):
    me, chan = lax.axis_index("seq"), lax.axis_index("chan")
    phase = lax.rem(me, 8)
    load_g = pltpu.make_async_copy(grads, g_here, in_sem.at[0])
    load_t = pltpu.make_async_copy(taps, t_here, in_sem.at[1])
    load_x = pltpu.make_async_copy(inputs, x_here, in_sem.at[2])
    barrier = pltpu.get_barrier_semaphore()

    def greet(to):
        pl.semaphore_signal(barrier, inc=1, device_id={"seq": to}, device_id_type=MESH)

    each_peer(me, greet)
    for step in (2, 1, 3):
        pl.semaphore_signal(barrier, inc=1, device_id={"chan": lax.rem(chan + step, CHAN_DEV)}, device_id_type=MESH)
    load_s = pltpu.make_async_copy(supports_far, supports, in_sem.at[3])
    load_t.start()
    load_g.start()
    load_s.start()
    load_x.start()

    lane_group, sublane = iota((8, 128), 1) // 16, iota((8, 128), 0)
    load_t.wait()
    for x in range(CHAN_DEV):
        t_rows[2 * x : 2 * x + 2, :] = t_here[:, x * WIDTH : (x + 1) * WIDTH]
    for tile in range(8):
        block = t_rows[:, tile * 128 : (tile + 1) * 128]
        skewed = block
        for r in range(1, 8):
            skewed = jnp.where(sublane == r, pltpu.roll(block, 128 - 16 * r, axis=1), skewed)
        moved = skewed
        for k in range(1, 8):
            moved = jnp.where(lane_group == k, pltpu.roll(skewed, k, axis=0), moved)
        row_send[tile * 8 : (tile + 1) * 8, :] = moved
    row_land[pl.ds(me, 1), :] = row_send[pl.ds(me, 1), :]
    load_g.wait()
    turn(g_here, g_send, False)
    g_land[me] = g_send[me]
    load_x.wait()
    turn(x_here, x_send, True)
    x_land[me] = x_send[me]
    pl.semaphore_wait(barrier, SEQ_DEV - 1 + CHAN_DEV - 1)

    spread(row_send, row_land, send_sem.at[2], recv_sem.at[2], me)
    spread(g_send, g_land, send_sem.at[1], recv_sem.at[1], me)
    spread(x_send, x_land, send_sem.at[3], recv_sem.at[3], me)
    row = iota((512, 1), 0)
    lag_of = (row % 64) * 8 + row // 64
    order[...] = jnp.where(iota((512, LAGS), 1) == lag_of, 1.0, 0.0).astype(BF16)
    g_wide[ROWS:, :] = jnp.zeros((SMAX * OWN, 128), F32)
    load_s.wait()
    own_lags = TB * supports[chan * (WIDTH // 128) + me // 8]
    take_all(row_land, send_sem.at[2], recv_sem.at[2], SEQ_DEV - 1)
    landed = pltpu.roll(row_land[...], lax.rem(8 - phase, 8) * 16, axis=1)
    flipped = jnp.concatenate([landed, pltpu.roll(landed, 16, axis=1)], axis=0).T
    for x in range(CHAN_DEV):
        at = (8 - 2 * x) % 8 * 16
        tap_send[x] = flipped[at : at + 16]
    for step in (2, 1, 3):
        to = lax.rem(chan + step, CHAN_DEV)
        pltpu.make_async_remote_copy(
            tap_send.at[to], tap_land.at[chan], send_sem.at[0], recv_sem.at[0], device_id={"chan": to}, device_id_type=MESH
        ).start()
    tap_land[chan] = tap_send[chan]
    take_all(tap_land, send_sem.at[0], recv_sem.at[0], CHAN_DEV - 1)
    placed = jnp.concatenate([tap_land[x] for x in range(CHAN_DEV)], axis=1)
    both = jnp.dot(high_low(placed), order[...], preferred_element_type=F32)
    tap_lines[...] = jnp.where(iota((OWN, LAGS), 1) < own_lags, both[:OWN] + both[OWN:], 0.0)

    below = iota((TB, TB), 1) >= iota((TB, TB), 0)

    def build(c, carry):
        line = tap_lines[pl.ds(c, 1), :]
        before = jnp.zeros((TB, TB), F32)
        for j in range(SMAX + 1):
            if j < SMAX:
                now = jnp.broadcast_to(line[:, j * TB : (j + 1) * TB], (TB, TB))
                now = pltpu.roll(now, 0, axis=1, stride=1, stride_axis=0)
            else:
                now = jnp.zeros((TB, TB), F32)
            toeplitz[c, :, j * TB : (j + 1) * TB] = high_low(jnp.where(below, now, before))
            before = now
        return carry

    lax.fori_loop(0, OWN, build, 0, unroll=16)

    take_all(g_land, send_sem.at[1], recv_sem.at[1], SEQ_DEV - 1)
    g_wide[0:ROWS, :] = g_land[...].reshape(ROWS, 128).astype(F32)

    def signal_back(c, carry):
        for j in range(SMAX + 1):
            windows[c, :, j * TB : (j + 1) * TB] = g_wide[pl.ds(j * OWN + c, SEQ_DEV, stride=OWN), :].astype(BF16)
        both = lax.dot_general(windows[c], toeplitz[c], NT, preferred_element_type=F32)
        gi_wide[pl.ds(c, SEQ_DEV, stride=OWN), :] = both[:, :TB] + both[:, TB:]
        return carry

    lax.fori_loop(0, OWN, signal_back, 0, unroll=16)
    gi_send[...] = gi_wide[...].astype(BF16).reshape(SEQ_DEV, OWN, 128)
    spread(gi_send, gi_land, send_sem.at[4], recv_sem.at[4], me)
    gi_land[me] = gi_send[me]

    take_all(x_land, send_sem.at[3], recv_sem.at[3], SEQ_DEV - 1)
    x_wide[...] = x_land[...].reshape(ROWS, 128).astype(F32)
    inside = iota((TB, TB), 1) <= iota((TB, TB), 0)

    def lag_sums(c, carry):
        signal = x_wide[pl.ds(c, SEQ_DEV, stride=OWN), :].T.astype(BF16)
        after = None
        for j in range(SMAX, -1, -1):
            product = jnp.dot(signal, windows[c, :, j * TB : (j + 1) * TB], preferred_element_type=F32)
            now = pltpu.roll(product, 1, axis=1, stride=1, stride_axis=0)
            if j < SMAX:
                lined = jnp.where(inside, now, after)
                partial[j, pl.ds(c * 8, 8), :] = jnp.sum(lined.reshape(TB // 8, 8, TB), axis=0)
            after = now
        return carry

    lax.fori_loop(0, OWN, lag_sums, 0, unroll=16)
    blocks = []
    for j in range(SMAX):
        added = partial[j, pl.ds(0, OWN, stride=8), :]
        for q in range(1, 8):
            added = added + partial[j, pl.ds(q, OWN, stride=8), :]
        blocks.append(added)
    sums = jnp.concatenate(blocks, axis=1)
    sums = jnp.where(iota((OWN, LAGS), 1) < own_lags, sums, 0.0)
    both = lax.dot_general(high_low(sums), order[...], NT, preferred_element_type=F32)
    placed = both[:OWN] + both[OWN:]
    stacked = []
    for p in range(8):
        x = (8 - p) % 8 // 2
        stacked.append(placed[:, x * 128 : (x + 1) * 128] if p % 2 == 0 else jnp.zeros((OWN, 128), F32))
    flipped = jnp.concatenate(stacked, axis=0).T
    back = flipped[:64] + pltpu.roll(flipped[64:], 112, axis=1)
    back_send[...] = pltpu.roll(back, phase * 16, axis=1)
    def to_owners(to):
        for step in (2, 1, 3, 0):
            other = lax.rem(chan + step, CHAN_DEV)
            pltpu.make_async_remote_copy(
                back_send.at[pl.ds(to, 1)], gf_out.at[pl.ds(chan * SEQ_DEV + me, 1)], send_sem.at[5], recv_sem.at[5],
                device_id={"seq": to, "chan": other}, device_id_type=MESH,
            ).start()

    in_order(me, to_owners)
    for step in (2, 1, 3):
        other = lax.rem(chan + step, CHAN_DEV)
        pltpu.make_async_remote_copy(
            back_send.at[pl.ds(me, 1)], gf_out.at[pl.ds(chan * SEQ_DEV + me, 1)], send_sem.at[5], recv_sem.at[5],
            device_id={"chan": other}, device_id_type=MESH,
        ).start()
    keep = pltpu.make_async_copy(back_send.at[pl.ds(me, 1)], gf_out.at[pl.ds(chan * SEQ_DEV + me, 1)], keep_sem.at[0])
    keep.start()
    take_all(gi_land, send_sem.at[4], recv_sem.at[4], SEQ_DEV - 1)
    for tile in range(WIDTH // 128):
        rows = gi_land[tile * 8 : (tile + 1) * 8].reshape(128, 128)
        gi_here[:, tile * 128 : (tile + 1) * 128] = rows.astype(F32).T.astype(BF16)
    store = pltpu.make_async_copy(gi_here, gi_out, keep_sem.at[1])
    store.start()
    keep.wait()
    take_all(gf_out, send_sem.at[5], recv_sem.at[5], CHAN_DEV * SEQ_DEV - 1)
    store.wait()


def finish(gi_here, gf_rows, gi, gf, gf_here, sem):
    store = pltpu.make_async_copy(gi_here, gi, sem.at[0])
    store.start()
    group = iota((32, 128), 1) // 16
    for half in range(2):
        lag = 2 * lax.axis_index("chan") + half
        line = jnp.zeros((32, 128), F32)
        for a in range(8):
            line = jnp.where(group == ((a + 8 - lag) & 7), gf_rows[pl.ds(a, 32, stride=8), :], line)
        line = pltpu.roll(line, 16 * lag, axis=1)
        for tile in range(32):
            gf_here[half : half + 1, tile * 128 : (tile + 1) * 128] = line[tile : tile + 1, :]
    store_f = pltpu.make_async_copy(gf_here, gf, sem.at[1])
    store_f.start()
    store.wait()
    store_f.wait()


def body(inputs, grads, filter_taps, supports):
    anywhere = pl.BlockSpec(memory_space=pl.ANY)
    blocks = (SEQ_DEV, OWN, 128)
    gi, gf_rows = pl.pallas_call(
        kernel,
        out_shape=(pltpu.VMEM((TB, WIDTH), BF16), pltpu.VMEM((CHAN_DEV * SEQ_DEV, 128), F32)),
        in_specs=[anywhere] * 4,
        out_specs=(anywhere, anywhere),
        scratch_shapes=[
            pltpu.SMEM((32,), jnp.int32),
            pltpu.VMEM((TB, WIDTH), BF16),
            pltpu.VMEM((TB, WIDTH), BF16),
            pltpu.VMEM((2, CHAN_DEV * WIDTH), F32),
            pltpu.VMEM(blocks, BF16),
            pltpu.VMEM(blocks, BF16),
            pltpu.VMEM(blocks, BF16),
            pltpu.VMEM(blocks, BF16),
            pltpu.VMEM(blocks, BF16),
            pltpu.VMEM((CHAN_DEV, OWN, 128), F32),
            pltpu.VMEM((CHAN_DEV, OWN, 128), F32),
            pltpu.VMEM((8, WIDTH), F32),
            pltpu.VMEM((SEQ_DEV, 128), F32),
            pltpu.VMEM((SEQ_DEV, 128), F32),
            pltpu.VMEM((ROWS + SMAX * OWN, 128), F32),
            pltpu.VMEM((ROWS, 128), F32),
            pltpu.VMEM((ROWS, 128), F32),
            pltpu.VMEM((OWN, 2 * TB, SPAN), BF16),
            pltpu.VMEM((OWN, SEQ_DEV, SPAN), BF16),
            pltpu.VMEM((OWN, LAGS), F32),
            pltpu.VMEM((SMAX, OWN * 8, TB), F32),
            pltpu.VMEM((512, LAGS), BF16),
            pltpu.VMEM((SEQ_DEV, 128), F32),
            pltpu.VMEM(blocks, BF16),
            pltpu.VMEM((TB, WIDTH), BF16),
            pltpu.SemaphoreType.DMA((4,)),
            pltpu.SemaphoreType.DMA((6,)),
            pltpu.SemaphoreType.DMA((6,)),
            pltpu.SemaphoreType.DMA((2,)),
        ],
        compiler_params=pltpu.CompilerParams(collective_id=0, has_side_effects=True, vmem_limit_bytes=48 * 2**20),
    )(*(pltpu.with_memory_space_constraint(a, pltpu.HBM) for a in (supports, grads, inputs, filter_taps)))
    return pl.pallas_call(
        finish,
        out_shape=(jax.ShapeDtypeStruct((TB, WIDTH), BF16), jax.ShapeDtypeStruct((2, CHAN_DEV * WIDTH), F32)),
        in_specs=[pl.BlockSpec(memory_space=pltpu.VMEM)] * 2,
        out_specs=(anywhere, anywhere),
        scratch_shapes=[pltpu.VMEM((2, CHAN_DEV * WIDTH), F32), pltpu.SemaphoreType.DMA((2,))],
        compiler_params=pltpu.CompilerParams(vmem_limit_bytes=8 * 2**20),
    )(gi, gf_rows)


def solution(mesh):
    in_specs = (P("seq", "chan"), P("seq", "chan"), P(("seq", "chan"), None), P())
    out_specs = (P("seq", "chan"), P(("seq", "chan"), None))
    return jax.shard_map(body, mesh=mesh, in_specs=in_specs, out_specs=out_specs, check_vma=False)
```
